32 devices in a mesh: seq: 8 (over z, core), section: 4 (over y, x).
Axes of the slice: x: 2, y: 2, z: 4, core: 2. Of those that a mesh axis runs over, the one named last changes fastest.
Arguments:
- query: bfloat16 [4, 3072, 3072], P('section', 'seq'), may hold values from -24 to 24, as said below
- key: bfloat16 [4, 3072, 3072], P('section', 'seq'), may hold values from -24 to 24
- value: bfloat16 [4, 3072, 3072], P('section', 'seq'), may hold values from -6 to 6
- cotangent: bfloat16 [4, 3072, 3072], P('section', 'seq'), may hold values from -96 to 96
- adjacency: int32 [24, 9], P('seq'), may hold values from 0 to 1, as said below
Outputs:
- gradients: bfloat16 [4, 3072, 3, 3072], P('section', 'seq')
The draws below stay inside these ranges and needn't reach their ends.
Inputs may be any that keep to these rules, and one draw needn't show every extreme that they name: query and key are drawn together. `adjacency`: the tile relation is symmetric: query tile a attends key tile b exactly when query tile b attends key tile a; every tile attends itself.
All inputs are finite; a program needn't handle non-finite values.
Results may differ from the reference program's by a relative error of at most 0.009.
Values may be sent and summed in bfloat16 or wider, within the bound.
No kernel may reach another device: no remote copies, remote signals or barrier semaphores. Data moves between devices by JAX's collectives and lax.ppermute only.
A program may use at most 128 MiB of HBM per device.

```python
import jax
import jax.numpy as jnp
from jax import lax

HEADS = 24
HD = 128
TILE = 128
TOK_DEV = 384
TOKENS = 3072
SECTIONS = 4


def pair_draw(key):
    base = jax.random.fold_in(key, 7)
    key_query, key_keys = jax.random.split(base, 2)
    shape = (SECTIONS, TOKENS, HEADS * HD)
    queries = jnp.clip(jax.random.normal(key_query, shape, jnp.float32), -4.0, 4.0)
    keys = jnp.clip(jax.random.normal(key_keys, shape, jnp.float32), -4.0, 4.0)
    return (queries.astype(jnp.bfloat16), keys.astype(jnp.bfloat16))


def draw_query(key, part):
    return pair_draw(key)[0]


def draw_key(key, part):
    return pair_draw(key)[1]


def draw_adjacency(key, part):
    tiles = TOKENS // TILE
    per_shard = TOK_DEV // TILE
    shards = TOKENS // TOK_DEV
    key_level, key_coin = jax.random.split(jax.random.fold_in(key, 13))
    levels = jax.random.randint(key_level, (tiles,), 1, 5)
    coins = jax.random.randint(key_coin, (tiles, tiles), 0, 8)
    rows = jnp.arange(tiles)[:, None]
    cols = jnp.arange(tiles)[None, :]
    coins = jnp.where(rows < cols, coins, coins.T)
    links = (coins < levels[:, None] + levels[None, :]) | (rows == cols)
    slots = jnp.arange(3 * per_shard)[None, :]
    target = (rows // per_shard + slots // per_shard - 1) % shards * per_shard + slots % per_shard
    return jnp.take_along_axis(links, target, axis=1).astype(jnp.int32)


def steps_of(stream_key, extent, cuts, low, top_value):
    factor_of = 1.0
    for axis_at, blocks in cuts:
        steps = jax.random.uniform(jax.random.fold_in(jax.random.fold_in(stream_key, 6), axis_at), (blocks,), jnp.float32, low / len(cuts), top_value / len(cuts))
        factor_of = factor_of * jnp.repeat(jnp.exp(steps), extent[axis_at] // blocks).reshape((-1,) + (1,) * (len(extent) - 1 - axis_at))
    return factor_of


def centred(key, dims, spread, limit, cuts=(), dtype=jnp.bfloat16):
    loudness = steps_of(key, dims, cuts, -0.22, 0.18) if cuts else 1.0
    entries = jax.random.normal(key, dims, jnp.float32) * spread * loudness
    return jnp.minimum(jnp.maximum(entries, -limit), limit).astype(dtype)


def setup_inputs(seed: int = 0) -> dict:
    seeds = jax.random.split(jax.random.key(seed), 6)
    return {
        "query": draw_query(jax.random.fold_in(seeds[5], 71), 0),
        "key": draw_key(jax.random.fold_in(seeds[5], 71), 0),
        "value": centred(seeds[2], (SECTIONS, TOKENS, HEADS * HD), 1.0, 6.0, ((0, 4), (1, 8))),
        "cotangent": centred(seeds[3], (SECTIONS, TOKENS, HEADS * HD), 16.0, 96.0, ((0, 4), (1, 8))),
        "adjacency": draw_adjacency(jax.random.fold_in(seeds[5], 71), 0),
    }


def shard_terms(queries, keys, values, cotangent, mask):
    scale = HD ** -0.5
    q_full = queries.astype(jnp.float32)
    k_full = keys.astype(jnp.float32)
    v_full = values.astype(jnp.float32)
    o_full = cotangent.astype(jnp.float32)
    scores = jnp.einsum("rhc,khc->hrk", q_full, k_full) * scale
    scores = jnp.where(mask[None], scores, -jnp.inf)
    top = jnp.max(scores, axis=2)
    weight = jnp.exp(scores - top[:, :, None])
    total = jnp.sum(weight, axis=2)
    prob = weight / total[:, :, None]
    prob_half = lax.optimization_barrier(prob.astype(jnp.bfloat16)).astype(jnp.float32)
    output = jnp.einsum("hrk,khc->rhc", prob_half, v_full)
    delta = jnp.einsum("rhc,rhc->hr", o_full, output)
    dprob = jnp.einsum("rhc,khc->hrk", o_full, v_full)
    dscore = lax.optimization_barrier((prob * (dprob - delta[:, :, None])).astype(jnp.bfloat16)).astype(jnp.float32)
    grad_query = jnp.einsum("hrk,khc->rhc", dscore, k_full) * scale
    part_key = jnp.einsum("hrk,rhc->khc", dscore, q_full) * scale
    part_value = jnp.einsum("hrk,rhc->khc", prob_half, o_full)
    return grad_query.astype(jnp.bfloat16), part_key.astype(jnp.bfloat16), part_value.astype(jnp.bfloat16)


def reference(query, key, value, cotangent, adjacency):
    shards = TOKENS // TOK_DEV
    per_shard = TOK_DEV // TILE
    full_width = HEADS * HD
    blocks = adjacency.reshape(shards, per_shard, 3 * per_shard)
    masks = jnp.broadcast_to(blocks[:, :, None, :, None] > 0, (shards, per_shard, TILE, 3 * per_shard, TILE))
    masks = masks.reshape(shards, TOK_DEV, 3 * TOK_DEV)

    def owners(part):
        part = part.astype(jnp.float32).reshape(shards, 3, TOK_DEV, full_width)
        summed = jnp.roll(part[:, 0], -1, 0) + part[:, 1] + jnp.roll(part[:, 2], 1, 0)
        return summed.astype(jnp.bfloat16).reshape(TOKENS, full_width)

    results = []
    for section in range(SECTIONS):
        queries = query[section].reshape(shards, TOK_DEV, HEADS, HD)
        keys = key[section].reshape(shards, TOK_DEV, HEADS, HD)
        values = value[section].reshape(shards, TOK_DEV, HEADS, HD)
        grads_out = cotangent[section].reshape(shards, TOK_DEV, HEADS, HD)
        window_keys = jnp.concatenate([jnp.roll(keys, 1, 0), keys, jnp.roll(keys, -1, 0)], axis=1)
        window_values = jnp.concatenate([jnp.roll(values, 1, 0), values, jnp.roll(values, -1, 0)], axis=1)
        grad_query, part_key, part_value = lax.map(
            lambda items: shard_terms(items[0], items[1], items[2], items[3], items[4]),
            (queries, window_keys, window_values, grads_out, masks))
        stacked = jnp.stack([grad_query.reshape(TOKENS, full_width), owners(part_key), owners(part_value)], axis=1)
        results.append(stacked)
    gathered = jnp.stack(results, 0)
    return jnp.roll(gathered, -1, 0)
```

```python
import functools
import math

import jax
import jax.numpy as jnp
from jax import lax
from jax.experimental import pallas as pl
from jax.experimental.pallas import tpu as pltpu
from jax.sharding import PartitionSpec as P

HD = 128
MASKED = 1e30
LOG2E = math.log2(math.e)
VMEM = 24 * 1024 * 1024


def nt(left, right):
    return lax.dot_general(left, right, (((1,), (1,)), ((), ())), preferred_element_type=jnp.float32)


def nn(left, right):
    return lax.dot_general(left, right, (((1,), (0,)), ((), ())), preferred_element_type=jnp.float32)


def stats_kernel(group, tiles, scale, bias, q_own, o_own, near, far, key, value, st_near, st_own, st_far):
    head = pl.program_id(0)
    keys = key[0]
    values = value[0]
    tile = keys.shape[0] // tiles
    windows = ((near[0], near[1], st_near), (q_own[0], o_own[0], st_own), (far[0], far[1], st_far))
    for w, (queries, grads, out) in enumerate(windows):
        scores = nt(keys, queries)
        dprob = nt(values, grads)
        shut = [bias[w * tiles + j : w * tiles + j + 1, :] for j in range(tiles)]
        parts = [scores[j * tile : (j + 1) * tile] for j in range(tiles)]
        top = None
        for j in range(tiles):
            best = jnp.max(parts[j], axis=0, keepdims=True) * scale - shut[j]
            top = best if top is None else jnp.maximum(top, best)
        total = jnp.zeros_like(top)
        moment = jnp.zeros_like(top)
        for j in range(tiles):
            row = jnp.where(shut[j] > 0.0, MASKED, top)
            weight = jnp.exp2(parts[j] * scale - row)
            total = total + jnp.sum(weight, axis=0, keepdims=True)
            moment = moment + jnp.sum(weight * dprob[j * tile : (j + 1) * tile], axis=0, keepdims=True)
        some = total > 0.0
        safe = jnp.where(some, total, 1.0)
        out[pl.ds(head, 1), :] = jnp.where(some, top + jnp.log2(safe), -MASKED)
        out[pl.ds(group + head, 1), :] = jnp.where(some, moment / safe, 0.0)


def grads_kernel(
    group, tiles, scale, out_scale, bias, q_own, o_own, near, far, key, value, st_near, st_own, st_far,
    dq_near, dq_own, dq_far, dkv, prob_all, dscore_all
):
    head = pl.program_id(0)
    keys = key[0]
    values = value[0]
    rows = keys.shape[0]
    tile = rows // tiles
    windows = ((near[0], near[1], st_near, dq_near), (q_own[0], o_own[0], st_own, dq_own), (far[0], far[1], st_far, dq_far))
    for w, (queries, grads, stat, dq) in enumerate(windows):
        scores = nt(keys, queries)
        dprob = nt(values, grads)
        lse = stat[pl.ds(head, 1), :]
        delta = stat[pl.ds(group + head, 1), :]
        for j in range(tiles):
            span = slice(j * tile, (j + 1) * tile)
            row = lse + bias[w * tiles + j : w * tiles + j + 1, :]
            prob = jnp.exp2(scores[span] * scale - row)
            prob_all[span, w * rows : (w + 1) * rows] = prob.astype(jnp.bfloat16)
            dscore_all[span, w * rows : (w + 1) * rows] = (prob * (dprob[span] - delta)).astype(jnp.bfloat16)
        back = lax.dot_general(
            dscore_all[:, w * rows : (w + 1) * rows], keys, (((0,), (0,)), ((), ())),
            preferred_element_type=jnp.float32,
        )
        dq[...] = (back * out_scale).astype(dq.dtype)
    dkey = None
    dvalue = None
    for w, (queries, grads, stat, dq) in enumerate(windows):
        part = nn(dscore_all[:, w * rows : (w + 1) * rows], queries)
        dkey = part if dkey is None else dkey + part
        part = nn(prob_all[:, w * rows : (w + 1) * rows], grads)
        dvalue = part if dvalue is None else dvalue + part
    dkv[0] = (dkey * out_scale).astype(jnp.bfloat16)
    dkv[1] = dvalue.astype(jnp.bfloat16)


def head_spec(rows, lead, first):
    return pl.BlockSpec((1, rows, HD), lambda h: (lead, 0, first + h))


def whole_spec(shape):
    return pl.BlockSpec(shape, lambda h: (0,) * len(shape))


def input_specs(bias, near, places, group):
    rows = near.shape[1]
    pair = pl.BlockSpec((2, rows, HD), lambda h: (0, 0, h))
    own = [head_spec(rows, lead, first) for lead, first in places]
    return [whole_spec(bias.shape), own[0], own[1], pair, pair, own[2], own[3]]


def window_stats(bias, arrays, places, near, far, group):
    rows = near.shape[1]
    tiles = bias.shape[0] // 3
    scale = HD ** (-0.5) * LOG2E
    stat = jax.ShapeDtypeStruct((2 * group, rows), jnp.float32)
    return pl.pallas_call(
        functools.partial(stats_kernel, group, tiles, scale),
        grid=(group,),
        in_specs=input_specs(bias, near, places, group),
        out_specs=[whole_spec(stat.shape)] * 3,
        out_shape=[stat] * 3,
        compiler_params=pltpu.CompilerParams(vmem_limit_bytes=VMEM),
        cost_estimate=pl.CostEstimate(
            flops=group * 2 * 2 * 3 * rows * rows * HD,
            bytes_accessed=group * 8 * rows * HD * 2,
            transcendentals=group * 3 * rows * rows,
        ),
        name="window_stats",
    )(bias, arrays[0], arrays[1], near, far, arrays[2], arrays[3])


def window_grads(bias, arrays, places, near, far, stats, group):
    rows = near.shape[1]
    tiles = bias.shape[0] // 3
    scale = HD ** (-0.5) * LOG2E
    width = group * HD
    flat = pl.BlockSpec((rows, HD), lambda h: (0, h))
    return pl.pallas_call(
        functools.partial(grads_kernel, group, tiles, scale, HD ** (-0.5)),
        grid=(group,),
        in_specs=input_specs(bias, near, places, group) + [whole_spec(stats[0].shape)] * 3,
        out_specs=[flat, flat, flat, pl.BlockSpec((2, rows, HD), lambda h: (0, 0, h))],
        out_shape=[
            jax.ShapeDtypeStruct((rows, width), jnp.bfloat16),
            jax.ShapeDtypeStruct((rows, width), jnp.float32),
            jax.ShapeDtypeStruct((rows, width), jnp.bfloat16),
            jax.ShapeDtypeStruct((2, rows, width), jnp.bfloat16),
        ],
        scratch_shapes=[pltpu.VMEM((rows, 3 * rows), jnp.bfloat16)] * 2,
        compiler_params=pltpu.CompilerParams(vmem_limit_bytes=VMEM),
        cost_estimate=pl.CostEstimate(
            flops=group * 5 * 2 * 3 * rows * rows * HD,
            bytes_accessed=group * 14 * rows * HD * 2,
            transcendentals=group * 3 * rows * rows,
        ),
        name="window_grads",
    )(bias, arrays[0], arrays[1], near, far, arrays[2], arrays[3], *stats)


def swap_near(block):
    size = lax.axis_size("seq")
    return lax.ppermute(block, "seq", [(i, i ^ 1) for i in range(size)])


def swap_far(block):
    size = lax.axis_size("seq")
    return lax.ppermute(block, "seq", [(i, (i + 1 if i % 2 else i - 1) % size) for i in range(size)])


def to_previous(block):
    size = lax.axis_size("section")
    return lax.ppermute(block, "section", [((i + 1) % size, i) for i in range(size)])


def merge(own, near, far, group):
    lse = [part[:group] for part in (own, near, far)]
    mean = [part[group:] for part in (own, near, far)]
    top = jnp.maximum(lse[0], jnp.maximum(lse[1], lse[2]))
    weight = [jnp.exp2(part - top) for part in lse]
    total = weight[0] + weight[1] + weight[2]
    delta = (weight[0] * mean[0] + weight[1] * mean[1] + weight[2] * mean[2]) / total
    return jnp.concatenate([top + jnp.log2(total), delta], 0)


def tile_bias(adjacency, tile):
    tiles = adjacency.shape[0]
    blocks = adjacency.reshape(tiles, 3, tiles)
    odd = lax.axis_index("seq") % 2 == 1
    near = jnp.where(odd, blocks[:, 0], blocks[:, 2])
    far = jnp.where(odd, blocks[:, 2], blocks[:, 0])
    flags = jnp.concatenate([near, blocks[:, 1], far], 0)
    bias = jnp.where(flags > 0, 0.0, MASKED).astype(jnp.float32)
    return jnp.repeat(bias, tile, axis=1)


def per_device(query, key, value, cotangent, adjacency):
    rows, width = query.shape[1:]
    heads = width // HD
    moved = heads // 6
    size = heads // 6
    first_moved = heads - moved
    local = [(s, min(size, first_moved - s)) for s in range(0, first_moved, size)]
    bias = tile_bias(adjacency, rows // adjacency.shape[0])

    def columns(array, first, count):
        return array[:, :, first * HD : (first + count) * HD]

    pairs = [jnp.concatenate([columns(query, s, n), columns(cotangent, s, n)], 0) for s, n in local]
    groups = [((query, cotangent, key, value), ((0, s),) * 4, n) for s, n in local]
    qd_moved = to_previous(jnp.concatenate([columns(query, first_moved, moved), columns(cotangent, first_moved, moved)], 0))
    kv_moved = to_previous(jnp.concatenate([columns(key, first_moved, moved), columns(value, first_moved, moved)], 0))
    pairs.append(qd_moved)
    groups.append(((qd_moved, qd_moved, kv_moved, kv_moved), ((0, 0), (1, 0), (0, 0), (1, 0)), moved))

    count = len(groups)
    near = [swap_near(pair) for pair in pairs]
    far = [swap_far(pair) for pair in pairs]
    out = jnp.zeros((3, rows, width), jnp.bfloat16)
    pieces = []
    for g in range(count):
        arrays, places, n = groups[g]
        st_near, st_own, st_far = window_stats(bias, arrays, places, near[g], far[g], n)
        own = merge(st_own, swap_near(st_near), swap_far(st_far), n)
        stats = (swap_near(own), own, swap_far(own))
        dq_near, dq_own, dq_far, dkv = window_grads(bias, arrays, places, near[g], far[g], stats, n)
        dq = dq_own + swap_near(dq_near).astype(jnp.float32) + swap_far(dq_far).astype(jnp.float32)
        dq = dq.astype(jnp.bfloat16)[None]
        if g < count - 1:
            dkv = to_previous(dkv)
            dq = to_previous(dq)
        pieces.append(jnp.concatenate([dq, dkv], 0))
    out = jnp.concatenate(pieces, 2)
    return jnp.transpose(out, (1, 0, 2))[None]


def solution(mesh):
    in_specs = (
        P("section", "seq", None),
        P("section", "seq", None),
        P("section", "seq", None),
        P("section", "seq", None),
        P("seq", None),
    )
    out_specs = P("section", "seq", None, None)
    return jax.shard_map(
        per_device, mesh=mesh, in_specs=in_specs, out_specs=out_specs, check_vma=False
    )
```

```python
import functools
import math

import jax
import jax.numpy as jnp
from jax import lax
from jax.experimental import pallas as pl
from jax.experimental.pallas import tpu as pltpu
from jax.sharding import PartitionSpec as P

HD = 128
MASKED = 1e30
STATS_STEP = 4
GRADS_STEP = 2
LOG2E = math.log2(math.e)
VMEM = 24 * 1024 * 1024


def nt(left, right):
    return lax.dot_general(left, right, (((1,), (1,)), ((), ())), preferred_element_type=jnp.float32)


def nn(left, right):
    return lax.dot_general(left, right, (((1,), (0,)), ((), ())), preferred_element_type=jnp.float32)


def gather_windows(all_rows, parts, lanes):
    rows = parts[0].shape[1]
    for w, part in enumerate(parts):
        all_rows[w * rows : (w + 1) * rows, :] = part[0, :, lanes]
    return all_rows[...]


def stats_kernel(group, tiles, scale, bias, q_own, o_own, q_near, o_near, far, key, value, st_near, st_own, st_far, q_all, o_all):
    rows = key.shape[1]
    tile = rows // tiles
    shut = [jnp.concatenate([bias[w * tiles + j : w * tiles + j + 1, :] for w in range(3)], 1) for j in range(tiles)]
    for at in range(STATS_STEP):
        head = pl.program_id(0) * STATS_STEP + at
        lanes = slice(at * HD, (at + 1) * HD)
        queries = gather_windows(q_all.at[at], (q_near, q_own, far.at[0:1]), lanes)
        grads = gather_windows(o_all.at[at], (o_near, o_own, far.at[1:2]), lanes)
        scores = nt(key[0, :, lanes], queries)
        dprob = nt(value[0, :, lanes], grads)
        parts = [scores[j * tile : (j + 1) * tile] for j in range(tiles)]
        top = None
        for j in range(tiles):
            best = jnp.max(parts[j], axis=0, keepdims=True) * scale - shut[j]
            top = best if top is None else jnp.maximum(top, best)
        total = jnp.zeros_like(top)
        moment = jnp.zeros_like(top)
        for j in range(tiles):
            row = jnp.where(shut[j] > 0.0, MASKED, top)
            weight = jnp.exp2(parts[j] * scale - row)
            total = total + jnp.sum(weight, axis=0, keepdims=True)
            moment = moment + jnp.sum(weight * dprob[j * tile : (j + 1) * tile], axis=0, keepdims=True)
        some = total > 0.0
        safe = jnp.where(some, total, 1.0)
        lse = jnp.where(some, top + jnp.log2(safe), -MASKED)
        mean = jnp.where(some, moment / safe, 0.0)
        for w, out in enumerate((st_near, st_own, st_far)):
            out[pl.ds(head, 1), :] = lse[:, w * rows : (w + 1) * rows]
            out[pl.ds(group + head, 1), :] = mean[:, w * rows : (w + 1) * rows]


def grads_kernel(
    group, tiles, scale, out_scale, bias, q_own, o_own, q_near, o_near, far, key, value, st_near, st_own, st_far,
    dq_near, dq_own, dq_far, dkv, prob_all, dscore_all, q_all, o_all
):
    rows = key.shape[1]
    tile = rows // tiles
    stats = (st_near, st_own, st_far)
    shut = [jnp.concatenate([bias[w * tiles + j : w * tiles + j + 1, :] for w in range(3)], 1) for j in range(tiles)]
    for at in range(GRADS_STEP):
        head = pl.program_id(0) * GRADS_STEP + at
        lanes = slice(at * HD, (at + 1) * HD)
        keys = key[0, :, lanes]
        queries = gather_windows(q_all.at[at], (q_near, q_own, far.at[0:1]), lanes)
        grads = gather_windows(o_all.at[at], (o_near, o_own, far.at[1:2]), lanes)
        lse = jnp.concatenate([stat[pl.ds(head, 1), :] for stat in stats], 1)
        delta = jnp.concatenate([stat[pl.ds(group + head, 1), :] for stat in stats], 1)
        scores = nt(keys, queries)
        dprob = nt(value[0, :, lanes], grads)
        for j in range(tiles):
            span = slice(j * tile, (j + 1) * tile)
            prob = jnp.exp2(scores[span] * scale - (lse + shut[j]))
            prob_all[at, span, :] = prob.astype(jnp.bfloat16)
            dscore_all[at, span, :] = (prob * (dprob[span] - delta)).astype(jnp.bfloat16)
        dscore = dscore_all[at]
        back = lax.dot_general(keys, dscore, (((0,), (0,)), ((), ())), preferred_element_type=jnp.float32) * out_scale
        back = jnp.transpose(back)
        for w, dq in enumerate((dq_near, dq_own, dq_far)):
            dq[:, lanes] = back[w * rows : (w + 1) * rows].astype(dq.dtype)
        dkv[0, :, lanes] = (nn(dscore, queries) * out_scale).astype(jnp.bfloat16)
        dkv[1, :, lanes] = nn(prob_all[at], grads).astype(jnp.bfloat16)


def head_spec(rows, step, lead, first):
    return pl.BlockSpec((1, rows, step * HD), lambda h: (lead, 0, first // step + h))


def whole_spec(shape):
    return pl.BlockSpec(shape, lambda h: (0,) * len(shape))


def input_specs(bias, far, places, step):
    rows = far.shape[1]
    pair = pl.BlockSpec((2, rows, step * HD), lambda h: (0, 0, h))
    return [whole_spec(bias.shape)] + [head_spec(rows, step, *place) for place in places[:4]] + [pair] + [
        head_spec(rows, step, *place) for place in places[4:]
    ]


def window_stats(bias, arrays, places, far, group):
    rows = far.shape[1]
    tiles = bias.shape[0] // 3
    scale = HD ** (-0.5) * LOG2E
    stat = jax.ShapeDtypeStruct((2 * group, rows), jnp.float32)
    return pl.pallas_call(
        functools.partial(stats_kernel, group, tiles, scale),
        grid=(group // STATS_STEP,),
        in_specs=input_specs(bias, far, places, STATS_STEP),
        out_specs=[whole_spec(stat.shape)] * 3,
        out_shape=[stat] * 3,
        scratch_shapes=[pltpu.VMEM((STATS_STEP, 3 * rows, HD), jnp.bfloat16)] * 2,
        compiler_params=pltpu.CompilerParams(vmem_limit_bytes=VMEM),
        cost_estimate=pl.CostEstimate(flops=int(1 * group * 4 * 3 * rows * rows * HD), bytes_accessed=1, transcendentals=0),
        name="window_stats",
    )(bias, *arrays[:4], far, *arrays[4:])


def window_grads(bias, arrays, places, far, stats, group):
    rows = far.shape[1]
    tiles = bias.shape[0] // 3
    scale = HD ** (-0.5) * LOG2E
    width = group * HD
    flat = pl.BlockSpec((rows, GRADS_STEP * HD), lambda h: (0, h))
    return pl.pallas_call(
        functools.partial(grads_kernel, group, tiles, scale, HD ** (-0.5)),
        grid=(group // GRADS_STEP,),
        in_specs=input_specs(bias, far, places, GRADS_STEP) + [whole_spec(stats[0].shape)] * 3,
        out_specs=[flat, flat, flat, pl.BlockSpec((2, rows, GRADS_STEP * HD), lambda h: (0, 0, h))],
        out_shape=[
            jax.ShapeDtypeStruct((rows, width), jnp.bfloat16),
            jax.ShapeDtypeStruct((rows, width), jnp.float32),
            jax.ShapeDtypeStruct((rows, width), jnp.bfloat16),
            jax.ShapeDtypeStruct((2, rows, width), jnp.bfloat16),
        ],
        scratch_shapes=[pltpu.VMEM((GRADS_STEP, rows, 3 * rows), jnp.bfloat16)] * 2
        + [pltpu.VMEM((GRADS_STEP, 3 * rows, HD), jnp.bfloat16)] * 2,
        compiler_params=pltpu.CompilerParams(vmem_limit_bytes=VMEM),
        cost_estimate=pl.CostEstimate(flops=int(1 * group * 10 * 3 * rows * rows * HD), bytes_accessed=1, transcendentals=0),
        name="window_grads",
    )(bias, *arrays[:4], far, *arrays[4:], *stats)


def swap_near(block, label="x"):
    size = lax.axis_size("seq")
    with jax.named_scope(label + "_near"):
      return lax.ppermute(block, "seq", [(i, i ^ 1) for i in range(size)])


def swap_far(block, label="x"):
    size = lax.axis_size("seq")
    with jax.named_scope(label + "_far"):
      return lax.ppermute(block, "seq", [(i, (i + 1 if i % 2 else i - 1) % size) for i in range(size)])


def to_previous(block, label="x"):
    size = lax.axis_size("section")
    with jax.named_scope(label + "_sec"):
      return lax.ppermute(block, "section", [((i + 1) % size, i) for i in range(size)])


def merge(own, near, far, group):
    lse = [part[:group] for part in (own, near, far)]
    mean = [part[group:] for part in (own, near, far)]
    top = jnp.maximum(lse[0], jnp.maximum(lse[1], lse[2]))
    weight = [jnp.exp2(part - top) for part in lse]
    total = weight[0] + weight[1] + weight[2]
    delta = (weight[0] * mean[0] + weight[1] * mean[1] + weight[2] * mean[2]) / total
    return jnp.concatenate([top + jnp.log2(total), delta], 0)


def tile_bias(adjacency, tile):
    tiles = adjacency.shape[0]
    blocks = adjacency.reshape(tiles, 3, tiles)
    odd = lax.axis_index("seq") % 2 == 1
    near = jnp.where(odd, blocks[:, 0], blocks[:, 2])
    far = jnp.where(odd, blocks[:, 2], blocks[:, 0])
    flags = jnp.concatenate([near, blocks[:, 1], far], 0)
    bias = jnp.where(flags > 0, 0.0, MASKED).astype(jnp.float32)
    return jnp.repeat(bias, tile, axis=1)


def after(block, *earlier):
    return lax.optimization_barrier((block, *earlier))[0]


def per_device(query, key, value, cotangent, adjacency):
    rows, width = query.shape[1:]
    heads = width // HD
    size = math.gcd(heads, 4)
    count = heads // size
    moved = count // 3
    local = count - moved
    bias = tile_bias(adjacency, rows // adjacency.shape[0])

    def columns(array, g):
        return array[:, :, g * size * HD : (g + 1) * size * HD]

    groups = []
    far, st, got, merged, stats, back, back_got, dkvs, dqs, four = ([None] * count for _ in range(10))
    token = [bias]

    def wait(*blocks):
        token.extend(blocks)

    def held(block):
        return after(block, *token)

    def near_far(near_block, far_block, label):
        near_got = swap_near(near_block, label)
        return near_got, swap_far(far_block, label)

    def send_in(g):
        if g >= local:
            block = held(four[g])[:2]
        else:
            block = jnp.concatenate([columns(held(query), g), columns(held(cotangent), g)], 0)
        far[g] = swap_far(block, f"in{g}")
        return block

    def move(g, *deps):
        block = jnp.concatenate([columns(held(array), g) for array in (query, cotangent, key, value)], 0)
        four[g] = to_previous(block, f"m{g}")

    def near_moved(g):
        mine = four[g]
        pair = swap_near(mine[:2], f"in{g}")
        groups.append(((mine, mine, pair, pair, mine, mine), ((0, 0), (1, 0), (0, 0), (1, 0), (2, 0), (3, 0))))

    def first(g):
        arrays, places = groups[g]
        st[g] = window_stats(held(bias), arrays, places, far[g], size)
        token[:] = [st[g][1]]
        got[g] = near_far(st[g][0], st[g][2], f"s1_{g}")

    def combine(g):
        merged[g] = merge(held(st[g][1]), *got[g], size)
        token[:] = [merged[g]]
        near_got, far_got = near_far(merged[g], merged[g], f"s2_{g}")
        stats[g] = (near_got, merged[g], far_got)

    def second(g):
        arrays, places = groups[g]
        dq_near, dq_own, dq_far, dkv = window_grads(held(bias), arrays, places, far[g], stats[g], size)
        token[:] = [dq_own]
        dkvs[g] = to_previous(dkv, f"dkv{g}") if g < local else dkv
        back[g] = (dq_near, dq_own, dq_far)

    def send_back(g):
        dq_near, dq_own, dq_far = back[g]
        back_got[g] = near_far(held(dq_near), held(dq_far), f"ret{g}")

    def finish(*gs):
        parts = []
        for g in gs:
            dq = held(back[g][1]) + back_got[g][0].astype(jnp.float32) + back_got[g][1].astype(jnp.float32)
            parts.append(dq.astype(jnp.bfloat16)[None])
        dq = jnp.concatenate(parts, 2)
        token[:] = [dq]
        if gs[0] < local:
            dq = to_previous(dq, f"dq{gs[0]}")
        for i, g in enumerate(gs):
            dqs[g] = dq[:, :, i * size * HD : (i + 1) * size * HD]

    m0, m1 = local, local + 1
    wait(send_in(0))
    q_near = swap_near(held(query), "q")
    o_near = swap_near(held(cotangent), "o")
    for g in range(local):
        groups.append(((query, cotangent, q_near, o_near, key, value), ((0, g * size),) * 6))
    move(m0)
    send_in(1)
    wait(q_near, o_near, far[0])
    first(0)
    wait(far[1], *got[0])
    combine(0)
    send_in(2)
    move(m1)
    first(1)
    wait(four[m0], *stats[0])
    send_in(3)
    second(0)
    wait(far[2], *got[1])
    combine(1)
    near_moved(m0)
    first(2)
    wait(far[3], *stats[1], *got[2])
    send_back(0)
    combine(2)
    wait(dkvs[0])
    first(3)
    wait(four[m1], groups[m0][0][2])
    send_in(m0)
    second(1)
    wait(*back_got[0], *stats[2], *got[3])
    combine(3)
    near_moved(m1)
    second(2)
    send_back(1)
    send_in(m1)
    wait(far[m0], *stats[3])
    second(3)
    send_back(2)
    wait(dkvs[1], *back_got[1])
    finish(0, 1)
    first(m0)
    wait(far[m1], *got[m0])
    combine(m0)
    first(m1)
    send_back(3)
    wait(*back_got[2], *stats[m0], *got[m1])
    combine(m1)
    wait(dkvs[2])
    second(m0)
    wait(*back_got[3])
    send_back(m0)
    finish(2, 3)
    wait(dkvs[3], *stats[m1])
    second(m1)
    send_back(m1)
    finish(m0)
    finish(m1)
    out = jnp.concatenate([jnp.concatenate([dqs[g], dkvs[g]], 0) for g in range(count)], 2)
    return jnp.transpose(out, (1, 0, 2))[None]


def solution(mesh):
    in_specs = (
        P("section", "seq", None),
        P("section", "seq", None),
        P("section", "seq", None),
        P("section", "seq", None),
        P("seq", None),
    )
    out_specs = P("section", "seq", None, None)
    return jax.shard_map(
        per_device, mesh=mesh, in_specs=in_specs, out_specs=out_specs, check_vma=False
    )
```

```python
import functools
import math

import jax
import jax.numpy as jnp
from jax import lax
from jax.experimental import pallas as pl
from jax.experimental.pallas import tpu as pltpu
from jax.sharding import PartitionSpec as P

HD = 128
MASKED = 1e30
STATS_STEP = 4
GRADS_STEP = 2
LOG2E = math.log2(math.e)
VMEM = 24 * 1024 * 1024


def nt(left, right):
    return lax.dot_general(left, right, (((1,), (1,)), ((), ())), preferred_element_type=jnp.float32)


def nn(left, right):
    return lax.dot_general(left, right, (((1,), (0,)), ((), ())), preferred_element_type=jnp.float32)


def gather_windows(all_rows, parts, lanes):
    rows = parts[0].shape[1]
    for w, part in enumerate(parts):
        all_rows[w * rows : (w + 1) * rows, :] = part[0, :, lanes]
    return all_rows[...]


def stats_kernel(group, tiles, scale, bias, q_own, o_own, q_near, o_near, far, key, value, st_near, st_own, st_far, q_all, o_all):
    rows = key.shape[1]
    tile = rows // tiles
    shut = [jnp.concatenate([bias[w * tiles + j : w * tiles + j + 1, :] for w in range(3)], 1) for j in range(tiles)]
    for at in range(STATS_STEP):
        head = pl.program_id(0) * STATS_STEP + at
        lanes = slice(at * HD, (at + 1) * HD)
        queries = gather_windows(q_all.at[at], (q_near, q_own, far.at[0:1]), lanes)
        grads = gather_windows(o_all.at[at], (o_near, o_own, far.at[1:2]), lanes)
        scores = nt(key[0, :, lanes], queries)
        dprob = nt(value[0, :, lanes], grads)
        parts = [scores[j * tile : (j + 1) * tile] for j in range(tiles)]
        top = None
        for j in range(tiles):
            best = jnp.max(parts[j], axis=0, keepdims=True) * scale - shut[j]
            top = best if top is None else jnp.maximum(top, best)
        total = jnp.zeros_like(top)
        moment = jnp.zeros_like(top)
        for j in range(tiles):
            row = jnp.where(shut[j] > 0.0, MASKED, top)
            weight = jnp.exp2(parts[j] * scale - row)
            total = total + jnp.sum(weight, axis=0, keepdims=True)
            moment = moment + jnp.sum(weight * dprob[j * tile : (j + 1) * tile], axis=0, keepdims=True)
        some = total > 0.0
        safe = jnp.where(some, total, 1.0)
        lse = jnp.where(some, top + jnp.log2(safe), -MASKED)
        mean = jnp.where(some, moment / safe, 0.0)
        for w, out in enumerate((st_near, st_own, st_far)):
            out[pl.ds(head, 1), :] = lse[:, w * rows : (w + 1) * rows]
            out[pl.ds(group + head, 1), :] = mean[:, w * rows : (w + 1) * rows]


def grads_kernel(
    group, tiles, scale, out_scale, bias, q_own, o_own, q_near, o_near, far, key, value, st_near, st_own, st_far,
    dq_near, dq_own, dq_far, dkv, prob_all, dscore_all, q_all, o_all
):
    rows = key.shape[1]
    tile = rows // tiles
    stats = (st_near, st_own, st_far)
    shut = [jnp.concatenate([bias[w * tiles + j : w * tiles + j + 1, :] for w in range(3)], 1) for j in range(tiles)]
    for at in range(GRADS_STEP):
        head = pl.program_id(0) * GRADS_STEP + at
        lanes = slice(at * HD, (at + 1) * HD)
        keys = key[0, :, lanes]
        queries = gather_windows(q_all.at[at], (q_near, q_own, far.at[0:1]), lanes)
        grads = gather_windows(o_all.at[at], (o_near, o_own, far.at[1:2]), lanes)
        lse = jnp.concatenate([stat[pl.ds(head, 1), :] for stat in stats], 1)
        delta = jnp.concatenate([stat[pl.ds(group + head, 1), :] for stat in stats], 1)
        scores = nt(keys, queries)
        dprob = nt(value[0, :, lanes], grads)
        for j in range(tiles):
            span = slice(j * tile, (j + 1) * tile)
            prob = jnp.exp2(scores[span] * scale - (lse + shut[j]))
            prob_all[at, span, :] = prob.astype(jnp.bfloat16)
            dscore_all[at, span, :] = (prob * (dprob[span] - delta)).astype(jnp.bfloat16)
        dscore = dscore_all[at]
        back = lax.dot_general(keys, dscore, (((0,), (0,)), ((), ())), preferred_element_type=jnp.float32) * out_scale
        back = jnp.transpose(back)
        for w, dq in enumerate((dq_near, dq_own, dq_far)):
            dq[:, lanes] = back[w * rows : (w + 1) * rows].astype(dq.dtype)
        dkv[0, :, lanes] = (nn(dscore, queries) * out_scale).astype(jnp.bfloat16)
        dkv[1, :, lanes] = nn(prob_all[at], grads).astype(jnp.bfloat16)


def head_spec(rows, step, lead, first):
    return pl.BlockSpec((1, rows, step * HD), lambda h: (lead, 0, first // step + h))


def whole_spec(shape):
    return pl.BlockSpec(shape, lambda h: (0,) * len(shape))


def input_specs(bias, far, places, step):
    rows = far.shape[1]
    pair = pl.BlockSpec((2, rows, step * HD), lambda h: (0, 0, h))
    return [whole_spec(bias.shape)] + [head_spec(rows, step, *place) for place in places[:4]] + [pair] + [
        head_spec(rows, step, *place) for place in places[4:]
    ]


def window_stats(bias, arrays, places, far, group):
    rows = far.shape[1]
    tiles = bias.shape[0] // 3
    scale = HD ** (-0.5) * LOG2E
    stat = jax.ShapeDtypeStruct((2 * group, rows), jnp.float32)
    return pl.pallas_call(
        functools.partial(stats_kernel, group, tiles, scale),
        grid=(group // STATS_STEP,),
        in_specs=input_specs(bias, far, places, STATS_STEP),
        out_specs=[whole_spec(stat.shape)] * 3,
        out_shape=[stat] * 3,
        scratch_shapes=[pltpu.VMEM((STATS_STEP, 3 * rows, HD), jnp.bfloat16)] * 2,
        compiler_params=pltpu.CompilerParams(vmem_limit_bytes=VMEM),
        cost_estimate=pl.CostEstimate(flops=int(1 * group * 4 * 3 * rows * rows * HD), bytes_accessed=1, transcendentals=0),
        name="window_stats",
    )(bias, *arrays[:4], far, *arrays[4:])


def window_grads(bias, arrays, places, far, stats, group):
    rows = far.shape[1]
    tiles = bias.shape[0] // 3
    scale = HD ** (-0.5) * LOG2E
    width = group * HD
    flat = pl.BlockSpec((rows, GRADS_STEP * HD), lambda h: (0, h))
    return pl.pallas_call(
        functools.partial(grads_kernel, group, tiles, scale, HD ** (-0.5)),
        grid=(group // GRADS_STEP,),
        in_specs=input_specs(bias, far, places, GRADS_STEP) + [whole_spec(stats[0].shape)] * 3,
        out_specs=[flat, flat, flat, pl.BlockSpec((2, rows, GRADS_STEP * HD), lambda h: (0, 0, h))],
        out_shape=[
            jax.ShapeDtypeStruct((rows, width), jnp.bfloat16),
            jax.ShapeDtypeStruct((rows, width), jnp.float32),
            jax.ShapeDtypeStruct((rows, width), jnp.bfloat16),
            jax.ShapeDtypeStruct((2, rows, width), jnp.bfloat16),
        ],
        scratch_shapes=[pltpu.VMEM((GRADS_STEP, rows, 3 * rows), jnp.bfloat16)] * 2
        + [pltpu.VMEM((GRADS_STEP, 3 * rows, HD), jnp.bfloat16)] * 2,
        compiler_params=pltpu.CompilerParams(vmem_limit_bytes=VMEM),
        cost_estimate=pl.CostEstimate(flops=int(1 * group * 10 * 3 * rows * rows * HD), bytes_accessed=1, transcendentals=0),
        name="window_grads",
    )(bias, *arrays[:4], far, *arrays[4:], *stats)


def swap_near(block, label="x"):
    size = lax.axis_size("seq")
    with jax.named_scope(label + "_near"):
        return lax.ppermute(block, "seq", [(i, i ^ 1) for i in range(size)])


def swap_far(block, label="x"):
    size = lax.axis_size("seq")
    with jax.named_scope(label + "_far"):
        return lax.ppermute(block, "seq", [(i, (i + 1 if i % 2 else i - 1) % size) for i in range(size)])


def to_previous(block, label="x"):
    size = lax.axis_size("section")
    with jax.named_scope(label + "_sec"):
        return lax.ppermute(block, "section", [((i + 1) % size, i) for i in range(size)])


def merge(own, near, far, group):
    lse = [part[..., :group, :] for part in (own, near, far)]
    mean = [part[..., group:, :] for part in (own, near, far)]
    top = jnp.maximum(lse[0], jnp.maximum(lse[1], lse[2]))
    weight = [jnp.exp2(part - top) for part in lse]
    total = weight[0] + weight[1] + weight[2]
    delta = (weight[0] * mean[0] + weight[1] * mean[1] + weight[2] * mean[2]) / total
    return jnp.concatenate([top + jnp.log2(total), delta], -2)


def tile_bias(adjacency, tile):
    tiles = adjacency.shape[0]
    blocks = adjacency.reshape(tiles, 3, tiles)
    odd = lax.axis_index("seq") % 2 == 1
    near = jnp.where(odd, blocks[:, 0], blocks[:, 2])
    far = jnp.where(odd, blocks[:, 2], blocks[:, 0])
    flags = jnp.concatenate([near, blocks[:, 1], far], 0)
    bias = jnp.where(flags > 0, 0.0, MASKED).astype(jnp.float32)
    return jnp.repeat(bias, tile, axis=1)


def after(block, *earlier):
    return lax.optimization_barrier((block, *earlier))[0]


def per_device(query, key, value, cotangent, adjacency):
    rows, width = query.shape[1:]
    heads = width // HD
    size = math.gcd(heads, 4)
    count = heads // size
    moved = count // 3
    local = count - moved
    bias = tile_bias(adjacency, rows // adjacency.shape[0])

    def columns(array, g):
        return array[:, :, g * size * HD : (g + 1) * size * HD]

    groups = []
    far, st, got, merged, stats, back, back_got, dkvs, dqs, four = ([None] * count for _ in range(10))
    token = [bias]

    def wait(*blocks):
        token.extend(blocks)

    def held(block):
        return after(block, *token)

    def near_far(near_block, far_block, label):
        near_got = swap_near(near_block, label)
        return near_got, swap_far(far_block, label)

    def send_in(g):
        if g >= local:
            block = held(four[g])[:2]
        else:
            block = jnp.concatenate([columns(held(query), g), columns(held(cotangent), g)], 0)
        far[g] = swap_far(block, f"in{g}")
        return block

    def move(g, *deps):
        block = jnp.concatenate([columns(held(array), g) for array in (query, cotangent, key, value)], 0)
        four[g] = to_previous(block, f"m{g}")

    def near_moved(g):
        mine = four[g]
        pair = swap_near(mine[:2], f"in{g}")
        groups.append(((mine, mine, pair, pair, mine, mine), ((0, 0), (1, 0), (0, 0), (1, 0), (2, 0), (3, 0))))

    def first(g):
        arrays, places = groups[g]
        st[g] = window_stats(held(bias), arrays, places, far[g], size)
        token[:] = [st[g][1]]

    def offer(*gs):
        blocks = [jnp.stack([held(st[g][i]) for g in gs]) for i in (0, 2)]
        got[gs[0]] = near_far(blocks[0], blocks[1], f"s1_{gs[0]}")

    def combine(*gs):
        own = jnp.stack([held(st[g][1]) for g in gs])
        whole = merge(own, *got[gs[0]], size)
        token[:] = [whole]
        near_got, far_got = near_far(whole, whole, f"s2_{gs[0]}")
        for i, g in enumerate(gs):
            stats[g] = (near_got[i], whole[i], far_got[i])
        return near_got, far_got

    def second(g):
        arrays, places = groups[g]
        dq_near, dq_own, dq_far, dkv = window_grads(held(bias), arrays, places, far[g], stats[g], size)
        token[:] = [dq_own]
        dkvs[g] = to_previous(dkv, f"dkv{g}") if g < local else dkv
        back[g] = (dq_near, dq_own, dq_far)

    def send_back(*gs):
        parts = [jnp.concatenate([back[g][i] for g in gs], 1) for i in (0, 2)]
        back_got[gs[0]] = near_far(held(parts[0]), held(parts[1]), f"ret{gs[0]}")

    def finish(*gs):
        found = [back_got[g] for g in gs if back_got[g] is not None]
        own, near_got, far_got = (
            jnp.concatenate(parts, 1) for parts in ([back[g][1] for g in gs], [f[0] for f in found], [f[1] for f in found])
        )
        dq = held(own) + near_got.astype(jnp.float32) + far_got.astype(jnp.float32)
        dq = dq.astype(jnp.bfloat16)[None]
        token[:] = [dq]
        if gs[0] < local:
            dq = to_previous(dq, f"dq{gs[0]}")
        for i, g in enumerate(gs):
            dqs[g] = dq[:, :, i * size * HD : (i + 1) * size * HD]

    m0, m1 = local, local + 1
    wait(send_in(0))
    q_near = swap_near(held(query), "q")
    o_near = swap_near(held(cotangent), "o")
    for g in range(local):
        groups.append(((query, cotangent, q_near, o_near, key, value), ((0, g * size),) * 6))
    move(m0)
    send_in(1)
    wait(q_near, o_near, far[0])
    first(0)
    send_in(2)
    move(m1)
    wait(far[1])
    first(1)
    offer(0, 1)
    wait(four[m0], far[2], *got[0])
    wait(*combine(0, 1))
    send_in(3)
    near_moved(m0)
    second(0)
    second(1)
    send_back(0)
    first(2)
    wait(four[m1], far[3])
    near_moved(m1)
    first(3)
    offer(2, 3)
    wait(dkvs[0], *back_got[0], *got[2])
    wait(*combine(2, 3))
    send_in(m0)
    send_in(m1)
    second(2)
    second(3)
    send_back(1)
    wait(dkvs[1], far[m0])
    first(m0)
    wait(dkvs[2], far[m1])
    first(m1)
    offer(m0, m1)
    wait(*back_got[1])
    finish(0, 1)
    wait(*got[m0])
    wait(*combine(m0, m1))
    send_back(2, 3)
    wait(dkvs[3])
    second(m0)
    send_back(m0)
    second(m1)
    send_back(m1)
    wait(*back_got[2])
    finish(2, 3)
    finish(m0)
    finish(m1)
    out = jnp.concatenate([jnp.concatenate([dqs[g], dkvs[g]], 0) for g in range(count)], 2)
    return jnp.transpose(out, (1, 0, 2))[None]


def solution(mesh):
    in_specs = (
        P("section", "seq", None),
        P("section", "seq", None),
        P("section", "seq", None),
        P("section", "seq", None),
        P("seq", None),
    )
    out_specs = P("section", "seq", None, None)
    return jax.shard_map(
        per_device, mesh=mesh, in_specs=in_specs, out_specs=out_specs, check_vma=False
    )
```

```python
import functools
import math

import jax
import jax.numpy as jnp
from jax import lax
from jax.experimental import pallas as pl
from jax.experimental.pallas import tpu as pltpu
from jax.sharding import PartitionSpec as P

HD = 128
MASKED = 1e30
STATS_STEP = 4
GRADS_STEP = 2
LOG2E = math.log2(math.e)
VMEM = 24 * 1024 * 1024


def nt(left, right):
    return lax.dot_general(left, right, (((1,), (1,)), ((), ())), preferred_element_type=jnp.float32)


def nn(left, right):
    return lax.dot_general(left, right, (((1,), (0,)), ((), ())), preferred_element_type=jnp.float32)


def gather_windows(all_rows, parts, lanes):
    rows = parts[0].shape[1]
    for w, part in enumerate(parts):
        all_rows[w * rows : (w + 1) * rows, :] = part[0, :, lanes]
    return all_rows[...]


def stats_kernel(group, tiles, scale, bias, q_own, o_own, q_near, o_near, far, key, value, st_near, st_own, st_far, q_all, o_all):
    rows = key.shape[1]
    tile = rows // tiles
    shut = [jnp.concatenate([bias[w * tiles + j : w * tiles + j + 1, :] for w in range(3)], 1) for j in range(tiles)]
    for at in range(STATS_STEP):
        head = pl.program_id(0) * STATS_STEP + at
        lanes = slice(at * HD, (at + 1) * HD)
        queries = gather_windows(q_all.at[at], (q_near, q_own, far.at[0:1]), lanes)
        grads = gather_windows(o_all.at[at], (o_near, o_own, far.at[1:2]), lanes)
        scores = nt(key[0, :, lanes], queries)
        dprob = nt(value[0, :, lanes], grads)
        parts = [scores[j * tile : (j + 1) * tile] for j in range(tiles)]
        top = None
        for j in range(tiles):
            best = jnp.max(parts[j], axis=0, keepdims=True) * scale - shut[j]
            top = best if top is None else jnp.maximum(top, best)
        total = jnp.zeros_like(top)
        moment = jnp.zeros_like(top)
        for j in range(tiles):
            row = jnp.where(shut[j] > 0.0, MASKED, top)
            weight = jnp.exp2(parts[j] * scale - row)
            total = total + jnp.sum(weight, axis=0, keepdims=True)
            moment = moment + jnp.sum(weight * dprob[j * tile : (j + 1) * tile], axis=0, keepdims=True)
        some = total > 0.0
        safe = jnp.where(some, total, 1.0)
        lse = jnp.where(some, top + jnp.log2(safe), -MASKED)
        mean = jnp.where(some, moment / safe, 0.0)
        for w, out in enumerate((st_near, st_own, st_far)):
            out[pl.ds(head, 1), :] = lse[:, w * rows : (w + 1) * rows]
            out[pl.ds(group + head, 1), :] = mean[:, w * rows : (w + 1) * rows]


def grads_kernel(
    group, tiles, scale, out_scale, bias, q_own, o_own, q_near, o_near, far, key, value, st_near, st_own, st_far,
    dq_near, dq_own, dq_far, dkv, prob_all, dscore_all, q_all, o_all
):
    rows = key.shape[1]
    tile = rows // tiles
    stats = (st_near, st_own, st_far)
    shut = [jnp.concatenate([bias[w * tiles + j : w * tiles + j + 1, :] for w in range(3)], 1) for j in range(tiles)]
    for at in range(GRADS_STEP):
        head = pl.program_id(0) * GRADS_STEP + at
        lanes = slice(at * HD, (at + 1) * HD)
        keys = key[0, :, lanes]
        queries = gather_windows(q_all.at[at], (q_near, q_own, far.at[0:1]), lanes)
        grads = gather_windows(o_all.at[at], (o_near, o_own, far.at[1:2]), lanes)
        lse = jnp.concatenate([stat[pl.ds(head, 1), :] for stat in stats], 1)
        delta = jnp.concatenate([stat[pl.ds(group + head, 1), :] for stat in stats], 1)
        scores = nt(keys, queries)
        dprob = nt(value[0, :, lanes], grads)
        for j in range(tiles):
            span = slice(j * tile, (j + 1) * tile)
            prob = jnp.exp2(scores[span] * scale - (lse + shut[j]))
            prob_all[at, span, :] = prob.astype(jnp.bfloat16)
            dscore_all[at, span, :] = (prob * (dprob[span] - delta)).astype(jnp.bfloat16)
        dscore = dscore_all[at]
        back = lax.dot_general(keys, dscore, (((0,), (0,)), ((), ())), preferred_element_type=jnp.float32) * out_scale
        back = jnp.transpose(back)
        for w, dq in enumerate((dq_near, dq_own, dq_far)):
            dq[:, lanes] = back[w * rows : (w + 1) * rows].astype(dq.dtype)
        dkv[0, :, lanes] = (nn(dscore, queries) * out_scale).astype(jnp.bfloat16)
        dkv[1, :, lanes] = nn(prob_all[at], grads).astype(jnp.bfloat16)


def head_spec(rows, step, lead, first):
    return pl.BlockSpec((1, rows, step * HD), lambda h: (lead, 0, first // step + h))


def whole_spec(shape):
    return pl.BlockSpec(shape, lambda h: (0,) * len(shape))


def input_specs(bias, far, places, step):
    rows = far.shape[1]
    pair = pl.BlockSpec((2, rows, step * HD), lambda h: (0, 0, h))
    return [whole_spec(bias.shape)] + [head_spec(rows, step, *place) for place in places[:4]] + [pair] + [
        head_spec(rows, step, *place) for place in places[4:]
    ]


def window_stats(bias, arrays, places, far, group):
    rows = far.shape[1]
    tiles = bias.shape[0] // 3
    scale = HD ** (-0.5) * LOG2E
    stat = jax.ShapeDtypeStruct((2 * group, rows), jnp.float32)
    return pl.pallas_call(
        functools.partial(stats_kernel, group, tiles, scale),
        grid=(group // STATS_STEP,),
        in_specs=input_specs(bias, far, places, STATS_STEP),
        out_specs=[whole_spec(stat.shape)] * 3,
        out_shape=[stat] * 3,
        scratch_shapes=[pltpu.VMEM((STATS_STEP, 3 * rows, HD), jnp.bfloat16)] * 2,
        compiler_params=pltpu.CompilerParams(vmem_limit_bytes=VMEM),
        cost_estimate=pl.CostEstimate(flops=int(1 * group * 4 * 3 * rows * rows * HD), bytes_accessed=1, transcendentals=0),
        name="window_stats",
    )(bias, *arrays[:4], far, *arrays[4:])


def window_grads(bias, arrays, places, far, stats, group):
    rows = far.shape[1]
    tiles = bias.shape[0] // 3
    scale = HD ** (-0.5) * LOG2E
    width = group * HD
    flat = pl.BlockSpec((rows, GRADS_STEP * HD), lambda h: (0, h))
    return pl.pallas_call(
        functools.partial(grads_kernel, group, tiles, scale, HD ** (-0.5)),
        grid=(group // GRADS_STEP,),
        in_specs=input_specs(bias, far, places, GRADS_STEP) + [whole_spec(stats[0].shape)] * 3,
        out_specs=[flat, flat, flat, pl.BlockSpec((2, rows, GRADS_STEP * HD), lambda h: (0, 0, h))],
        out_shape=[
            jax.ShapeDtypeStruct((rows, width), jnp.bfloat16),
            jax.ShapeDtypeStruct((rows, width), jnp.float32),
            jax.ShapeDtypeStruct((rows, width), jnp.bfloat16),
            jax.ShapeDtypeStruct((2, rows, width), jnp.bfloat16),
        ],
        scratch_shapes=[pltpu.VMEM((GRADS_STEP, rows, 3 * rows), jnp.bfloat16)] * 2
        + [pltpu.VMEM((GRADS_STEP, 3 * rows, HD), jnp.bfloat16)] * 2,
        compiler_params=pltpu.CompilerParams(vmem_limit_bytes=VMEM),
        cost_estimate=pl.CostEstimate(flops=int(1 * group * 10 * 3 * rows * rows * HD), bytes_accessed=1, transcendentals=0),
        name="window_grads",
    )(bias, *arrays[:4], far, *arrays[4:], *stats)


def swap_near(block, label="x"):
    size = lax.axis_size("seq")
    with jax.named_scope(label + "_near"):
        return lax.ppermute(block, "seq", [(i, i ^ 1) for i in range(size)])


def swap_far(block, label="x"):
    size = lax.axis_size("seq")
    with jax.named_scope(label + "_far"):
        return lax.ppermute(block, "seq", [(i, (i + 1 if i % 2 else i - 1) % size) for i in range(size)])


def to_previous(block, label="x"):
    size = lax.axis_size("section")
    with jax.named_scope(label + "_sec"):
        return lax.ppermute(block, "section", [((i + 1) % size, i) for i in range(size)])


def merge(own, near, far, group):
    lse = [part[..., :group, :] for part in (own, near, far)]
    mean = [part[..., group:, :] for part in (own, near, far)]
    top = jnp.maximum(lse[0], jnp.maximum(lse[1], lse[2]))
    weight = [jnp.exp2(part - top) for part in lse]
    total = weight[0] + weight[1] + weight[2]
    delta = (weight[0] * mean[0] + weight[1] * mean[1] + weight[2] * mean[2]) / total
    return jnp.concatenate([top + jnp.log2(total), delta], -2)


def tile_bias(adjacency, tile):
    tiles = adjacency.shape[0]
    blocks = adjacency.reshape(tiles, 3, tiles)
    odd = lax.axis_index("seq") % 2 == 1
    near = jnp.where(odd, blocks[:, 0], blocks[:, 2])
    far = jnp.where(odd, blocks[:, 2], blocks[:, 0])
    flags = jnp.concatenate([near, blocks[:, 1], far], 0)
    bias = jnp.where(flags > 0, 0.0, MASKED).astype(jnp.float32)
    return jnp.repeat(bias, tile, axis=1)


def after(block, *earlier):
    return lax.optimization_barrier((block, *earlier))[0]


def per_device(query, key, value, cotangent, adjacency):
    rows, width = query.shape[1:]
    heads = width // HD
    size = math.gcd(heads, 4)
    count = heads // size
    moved = count // 3
    local = count - moved
    bias = tile_bias(adjacency, rows // adjacency.shape[0])

    def columns(array, g):
        return array[:, :, g * size * HD : (g + 1) * size * HD]

    groups = []
    far, st, got, merged, stats, back, back_got, dkvs, dqs, four = ([None] * count for _ in range(10))
    token = [bias]

    def wait(*blocks):
        token.extend(blocks)

    def held(block):
        return after(block, *token)

    def near_far(near_block, far_block, label):
        near_got = swap_near(near_block, label)
        return near_got, swap_far(far_block, label)

    def send_in(g):
        if g >= local:
            block = held(four[g])[:2]
        else:
            block = jnp.concatenate([columns(held(query), g), columns(held(cotangent), g)], 0)
        far[g] = swap_far(block, f"in{g}")
        return block

    def move(g, *deps):
        block = jnp.concatenate([columns(held(array), g) for array in (query, cotangent, key, value)], 0)
        four[g] = to_previous(block, f"m{g}")

    def near_moved(g):
        mine = four[g]
        pair = swap_near(mine[:2], f"in{g}")
        groups.append(((mine, mine, pair, pair, mine, mine), ((0, 0), (1, 0), (0, 0), (1, 0), (2, 0), (3, 0))))

    def first(g):
        arrays, places = groups[g]
        st[g] = window_stats(held(bias), arrays, places, far[g], size)
        token[:] = [st[g][1]]

    def offer(*gs):
        blocks = [jnp.stack([held(st[g][i]) for g in gs]) for i in (0, 2)]
        got[gs[0]] = near_far(blocks[0], blocks[1], f"s1_{gs[0]}")

    def combine(*gs):
        own = jnp.stack([held(st[g][1]) for g in gs])
        whole = merge(own, *got[gs[0]], size)
        token[:] = [whole]
        near_got, far_got = near_far(whole, whole, f"s2_{gs[0]}")
        for i, g in enumerate(gs):
            stats[g] = (near_got[i], whole[i], far_got[i])
        return near_got, far_got

    def second(g):
        arrays, places = groups[g]
        dq_near, dq_own, dq_far, dkv = window_grads(held(bias), arrays, places, far[g], stats[g], size)
        token[:] = [dq_own]
        dkvs[g] = to_previous(dkv, f"dkv{g}") if g < local else dkv
        back[g] = (dq_near, dq_own, dq_far)

    def send_back(*gs):
        parts = [jnp.concatenate([back[g][i] for g in gs], 1) for i in (0, 2)]
        back_got[gs[0]] = near_far(held(parts[0]), held(parts[1]), f"ret{gs[0]}")

    def finish(*gs):
        found = [back_got[g] for g in gs if back_got[g] is not None]
        own, near_got, far_got = (
            jnp.concatenate(parts, 1) for parts in ([back[g][1] for g in gs], [f[0] for f in found], [f[1] for f in found])
        )
        dq = held(own) + near_got.astype(jnp.float32) + far_got.astype(jnp.float32)
        dq = dq.astype(jnp.bfloat16)[None]
        token[:] = [dq]
        if gs[0] < local:
            dq = to_previous(dq, f"dq{gs[0]}")
        for i, g in enumerate(gs):
            dqs[g] = dq[:, :, i * size * HD : (i + 1) * size * HD]

    m0, m1 = local, local + 1
    wait(send_in(0))
    q_near = swap_near(held(query), "q")
    o_near = swap_near(held(cotangent), "o")
    for g in range(local):
        groups.append(((query, cotangent, q_near, o_near, key, value), ((0, g * size),) * 6))
    move(m0)
    send_in(1)
    wait(q_near, o_near, far[0])
    first(0)
    send_in(2)
    move(m1)
    wait(far[1])
    first(1)
    offer(0, 1)
    wait(four[m0], far[2], *got[0])
    wait(*combine(0, 1))
    send_in(3)
    near_moved(m0)
    second(0)
    second(1)
    send_back(0)
    first(2)
    wait(four[m1], far[3])
    near_moved(m1)
    first(3)
    offer(2, 3)
    wait(*back_got[0], *got[2])
    wait(*combine(2, 3))
    wait(dkvs[0])
    send_in(m0)
    send_in(m1)
    second(2)
    second(3)
    send_back(1)
    wait(dkvs[1], far[m0])
    first(m0)
    wait(dkvs[2], far[m1])
    first(m1)
    offer(m0, m1)
    wait(*back_got[1])
    finish(0, 1)
    wait(*got[m0])
    wait(*combine(m0, m1))
    send_back(2, 3)
    wait(dkvs[3])
    second(m0)
    send_back(m0)
    second(m1)
    send_back(m1)
    wait(*back_got[2])
    finish(2, 3)
    finish(m0)
    finish(m1)
    out = jnp.concatenate([jnp.concatenate([dqs[g], dkvs[g]], 0) for g in range(count)], 2)
    return jnp.transpose(out, (1, 0, 2))[None]


def solution(mesh):
    in_specs = (
        P("section", "seq", None),
        P("section", "seq", None),
        P("section", "seq", None),
        P("section", "seq", None),
        P("seq", None),
    )
    out_specs = P("section", "seq", None, None)
    return jax.shard_map(
        per_device, mesh=mesh, in_specs=in_specs, out_specs=out_specs, check_vma=False
    )
```
